512 devices in a mesh: dp: 32 (over y_lo, z), mp: 16 (over x, y_hi, core).
Axes of the slice: x: 4, y: 8 (y_hi: 2, y_lo: 4; y = y_hi * 4 + y_lo), z: 8, core: 2. Of those that a mesh axis runs over, the one named last changes fastest.
Arguments:
- tokens: bfloat16 [11776, 2048], P('dp', 'mp'), may hold values from -21 to 21, as said below
- cotangent: bfloat16 [11776, 5120], P('dp', 'mp'), may hold values from -8.7576054 to 8.7576054, as said below
- weights: float32 [2, 2048, 5120], P(None, 'dp', 'mp'), may hold values from -14 to 14, as said below
- row_moments: float32 [2, 2048], P(None, 'dp'), may hold values from 0.05 to 2
- col_moments: float32 [2, 5120], P(None, 'mp'), may hold values from 0.05 to 2
Outputs:
- input_grad: bfloat16 [11776, 2048], P('dp', 'mp')
- weight_step: float32 [2, 2048, 5120], P(None, 'dp', 'mp')
- new_rows: float32 [2, 2048], P(None, 'dp')
- new_cols: float32 [2, 5120], P(None, 'mp')
The draws below stay inside these ranges and needn't reach their ends.
Inputs may be any that keep to these rules, and one draw needn't show every extreme that they name: `tokens`: activations with a different scale for each feature. `cotangent`: gradients with a different scale for each hidden unit. weights of order one with a different scale for each row.
All inputs are finite; a program needn't handle non-finite values.
Results may differ from the reference program's by a relative error of at most 0.029.
Values may be sent and summed in bfloat16 or wider, within the bound.
No kernel may reach another device: no remote copies, remote signals or barrier semaphores. Data moves between devices by JAX's collectives and lax.ppermute only.
A program may use at most 64 MiB of HBM per device.

```python
import math
import jax
import jax.numpy as jnp
from jax import lax

D = 2048
FF = 5120
TOK_DEV = 368
TOKENS = 11776
N_DP = 32
N_MP = 16


def level_ramp(subkey, length, spread):
    jitter = jax.random.uniform(subkey, (length,), jnp.float32, -spread, spread)
    ramp = jnp.arange(length, dtype=jnp.float32) / length - 0.5
    return jnp.exp(ramp * math.log(3.0) + jitter)


def draw_tokens(key, part):
    key = jax.random.fold_in(key, 11)
    first_key, second_key = jax.random.split(key, 2)
    feature_levels = level_ramp(first_key, D, 1.1)
    entries = jnp.clip(jax.random.normal(second_key, (TOKENS, D), jnp.float32), -4.0, 4.0)
    result = entries * feature_levels[None, :]
    return result.astype(jnp.bfloat16)


def draw_cotangent(key, part):
    key = jax.random.fold_in(key, 23)
    first_key, second_key = jax.random.split(key, 2)
    column_levels = level_ramp(first_key, FF, 1.1) * math.sqrt(D / TOKENS)
    entries = jnp.clip(jax.random.normal(second_key, (TOKENS, FF), jnp.float32), -4.0, 4.0)
    return (entries * column_levels[None, :]).astype(jnp.bfloat16)


def draw_weights(key, part):
    key = jax.random.fold_in(key, 37)
    first_key, second_key, third_key = jax.random.split(key, 3)
    levels_gate = level_ramp(first_key, D, 0.7)
    levels_up = level_ramp(third_key, D, 0.7)
    row_levels = jnp.stack([levels_gate, levels_up])[:, :, None]
    entries = jnp.clip(jax.random.normal(second_key, (2, D, FF), jnp.float32), -4.0, 4.0)
    return entries * row_levels


def level_of(own_key, shape, cuts, low, top_value):
    def one(dim, blocks):
        heights = jax.random.uniform(jax.random.fold_in(jax.random.fold_in(own_key, 6), dim), (blocks,), jnp.float32, low / len(cuts), top_value / len(cuts))
        return jnp.repeat(jnp.exp(heights), shape[dim] // blocks).reshape((-1,) + (1,) * (len(shape) - dim - 1))

    loudness = one(*cuts[0])
    for cut in cuts[1:]:
        loudness = loudness * one(*cut)
    return loudness


def setup_inputs(seed: int = 0) -> dict:
    arg_keys = jax.random.split(jax.random.key(seed), 6)
    return {
        "tokens": draw_tokens(jax.random.fold_in(arg_keys[5], 71), 0),
        "cotangent": draw_cotangent(jax.random.fold_in(arg_keys[5], 71), 0),
        "weights": draw_weights(jax.random.fold_in(arg_keys[5], 71), 0),
        "row_moments": jnp.clip(jnp.exp(math.log(2.0) - 3.6888794 * jax.random.uniform(arg_keys[3], (2, D), jnp.float32) ** level_of(arg_keys[3], (2, D), ((1, 32),), -0.2, 0.2)), 0.05, 2.0),
        "col_moments": jnp.clip(jnp.exp(math.log(2.0) - 3.6888794 * jax.random.uniform(arg_keys[4], (2, FF), jnp.float32) ** level_of(arg_keys[4], (2, FF), ((1, 16),), -0.2, 0.2)), 0.05, 2.0),
    }


def gelu_parts(values):
    cubed_values = values * values * values
    argument = 0.7978845608 * (values + 0.044715 * cubed_values)
    tangent = jnp.tanh(argument)
    gelu_value = 0.5 * values * (1.0 + tangent)
    gelu_slope = 0.5 * (1.0 + tangent) + 0.5 * values * (1.0 - tangent * tangent) * 0.7978845608 * (1.0 + 3.0 * 0.044715 * values * values)
    return (gelu_value, gelu_slope)

def reference(tokens, cotangent, weights, row_moments, col_moments):
    scaling = D ** (-0.5)
    weights_half = weights.astype(jnp.bfloat16)
    preact = jnp.einsum('td,kdf->ktf', tokens.astype(jnp.float32), weights_half.astype(jnp.float32)) * scaling
    gelu_value, gelu_slope = gelu_parts(preact[0])
    grad_gate = (cotangent.astype(jnp.float32) * preact[1] * gelu_slope).astype(jnp.bfloat16)
    grad_up = (cotangent.astype(jnp.float32) * gelu_value).astype(jnp.bfloat16)
    hidden_grads = jnp.stack([grad_gate, grad_up])
    token_groups = tokens.reshape(N_DP, TOK_DEV, D)
    grad_groups = hidden_grads.reshape(2, N_DP, TOK_DEV, FF).transpose(1, 0, 2, 3)

    def add_group(running, inputs):
        group_tokens, group_grads = inputs
        partial_value = jnp.einsum('td,ktf->kdf', group_tokens.astype(jnp.float32), group_grads.astype(jnp.float32)) * scaling
        rounded = lax.optimization_barrier(partial_value.astype(jnp.bfloat16))
        return (running + rounded.astype(jnp.float32), None)
    weight_grads, _ = lax.scan(add_group, jnp.zeros((2, D, FF), jnp.float32), (token_groups, grad_groups))
    block_width = FF // N_MP

    def add_block(running, position):
        offset = (position * block_width).astype(jnp.int32)
        grads_block = lax.dynamic_slice_in_dim(hidden_grads, offset, block_width, 2)
        weights_block = lax.dynamic_slice_in_dim(weights_half, offset, block_width, 2)
        partial_value = jnp.einsum('ktf,kdf->td', grads_block.astype(jnp.float32), weights_block.astype(jnp.float32)) * scaling
        rounded = lax.optimization_barrier(partial_value.astype(jnp.bfloat16))
        return (running + rounded.astype(jnp.float32), None)
    input_total, _ = lax.scan(add_block, jnp.zeros((TOKENS, D), jnp.float32), jnp.arange(N_MP, dtype=jnp.int32))
    input_grad = input_total.astype(jnp.bfloat16)
    squares = weight_grads * weight_grads + 1e-30
    new_rows = 0.5 * row_moments + 0.5 * lax.optimization_barrier(jnp.mean(squares, axis=2))
    new_cols = 0.5 * col_moments + 0.5 * lax.optimization_barrier(jnp.mean(squares, axis=1))
    row_level = lax.optimization_barrier(jnp.mean(new_rows, axis=1))
    estimate = new_rows[:, :, None] * new_cols[:, None, :] / row_level[:, None, None]
    update = weight_grads * lax.rsqrt(estimate)
    step_scale = jnp.sqrt(lax.optimization_barrier(jnp.mean(weights * weights, axis=(1, 2))))
    weight_step = step_scale[:, None, None] * update
    return (input_grad, weight_step, new_rows, new_cols)
```

```python
import functools
import jax
import jax.numpy as jnp
from jax import lax
from jax.experimental import pallas as pl
from jax.experimental.pallas import tpu as pltpu
from jax.sharding import Mesh, PartitionSpec as P

D = 2048
FF = 5120
N_YLO, N_Z, N_X, N_YHI, N_CORE = 4, 8, 4, 2, 2
N_DP = N_YLO * N_Z
N_MP = N_X * N_YHI * N_CORE
N_XY = N_X * N_YHI
TOK = 368
ROWS = D // N_DP
COLS = FF // N_MP
FEAT = D // N_MP
SCALING = D ** (-0.5)
DP = ("ylo", "z")
XY = ("x", "yhi")
MP = ("x", "yhi", "core")
F32 = jnp.float32
BF16 = jnp.bfloat16


def gelu_parts(values):
    cubed_values = values * values * values
    argument = 0.7978845608 * (values + 0.044715 * cubed_values)
    tangent = jnp.tanh(argument)
    gelu_value = 0.5 * values * (1.0 + tangent)
    gelu_slope = 0.5 * (1.0 + tangent) + 0.5 * values * (1.0 - tangent * tangent) * 0.7978845608 * (
        1.0 + 3.0 * 0.044715 * values * values
    )
    return (gelu_value, gelu_slope)


def weight_block(w_ref, s):
    ylo, z = s // 4, 2 * (s % 4)
    return jnp.concatenate([w_ref[z, ylo], w_ref[z + 1, ylo]], axis=0)


def grads_kernel(tok_ref, w_ref, cot_ref, grads_ref, hidden_ref):
    acc = jnp.zeros((TOK, 2 * COLS), F32)
    for s in range(0, N_MP, 2):
        left = jnp.concatenate([tok_ref[0, s // 2], tok_ref[1, s // 2]], axis=1)
        right = jnp.concatenate([weight_block(w_ref, s), weight_block(w_ref, s + 1)], axis=0)
        acc = acc + jnp.dot(left, right, preferred_element_type=F32)
    acc = acc * SCALING
    gelu_value, gelu_slope = gelu_parts(acc[:, :COLS])
    cot = cot_ref[...].astype(F32)
    hidden_ref[:, :COLS] = (cot * acc[:, COLS:] * gelu_slope).astype(BF16)
    hidden_ref[:, COLS:] = (cot * gelu_value).astype(BF16)
    hidden = hidden_ref[...]
    for s in range(0, N_MP, 2):
        left = jnp.concatenate([tok_ref[0, s // 2], tok_ref[1, s // 2]], axis=1)
        product = lax.dot_general(left, hidden, (((0,), (0,)), ((), ())), preferred_element_type=F32)
        product = (product * SCALING).astype(BF16)
        ylo, z = s // 4, 2 * (s % 4)
        for part in range(4):
            grads_ref[z + part, ylo] = product[part * ROWS : (part + 1) * ROWS]


def input_kernel(hidden_ref, w_ref, out_ref):
    hidden = hidden_ref[...]
    for s in range(0, N_MP, 2):
        right = jnp.concatenate([weight_block(w_ref, s), weight_block(w_ref, s + 1)], axis=0)
        product = lax.dot_general(hidden, right, (((1,), (1,)), ((), ())), preferred_element_type=F32)
        product = (product * SCALING).astype(BF16)
        out_ref[0, s // 2] = product[:, :FEAT]
        out_ref[1, s // 2] = product[:, FEAT:]


def call(kernel, out_shape, flops, *args):
    vmem = pl.BlockSpec(memory_space=pltpu.VMEM)
    return pl.pallas_call(
        kernel,
        out_shape=out_shape,
        in_specs=[vmem] * len(args),
        out_specs=jax.tree.map(lambda _: vmem, out_shape),
        compiler_params=pltpu.CompilerParams(vmem_limit_bytes=40 * 2**20),
        cost_estimate=pl.CostEstimate(flops=flops, bytes_accessed=8 * 2**20, transcendentals=0),
    )(*args)


def spread(values, axis, size):
    return lax.all_to_all(jnp.broadcast_to(values[None], (size,) + values.shape), axis, 0, 0, tiled=True)


def shards(tokens, cotangent, weights, row_moments, col_moments):
    half = weights.astype(BF16)
    half = jnp.concatenate([half[0], half[1]], axis=1)
    some_rows = spread(half, "ylo", N_YLO)
    full = lax.all_gather(some_rows, "z", axis=0)
    features = spread(tokens, XY, N_XY)
    features = lax.all_gather(features, "core", axis=0)
    flops = 2 * TOK * D * 2 * COLS
    grads, hidden = call(
        grads_kernel,
        [jax.ShapeDtypeStruct((N_Z, N_YLO, ROWS, 2 * COLS), BF16), jax.ShapeDtypeStruct((TOK, 2 * COLS), BF16)],
        2 * flops, features, full, cotangent,
    )
    some_grads = lax.psum_scatter(grads, "z", scatter_dimension=0, tiled=False)
    terms = call(
        input_kernel, jax.ShapeDtypeStruct((N_CORE, N_XY, TOK, FEAT), BF16), flops, hidden, full
    )
    terms = lax.all_to_all(terms, "core", 0, 0, tiled=True)
    terms = (terms[0].astype(F32) + terms[1].astype(F32)).astype(BF16)
    terms = lax.all_to_all(terms, XY, 0, 0, tiled=True)
    input_grad = jnp.sum(terms.astype(F32), axis=0).astype(BF16)

    own = jnp.sum(lax.all_to_all(some_grads, "ylo", 0, 0, tiled=True).astype(F32), axis=0)
    squares = own * own + 1e-30
    col_part = jnp.sum(squares, axis=0)
    row_part = jnp.stack([jnp.sum(squares[:, :COLS], axis=1), jnp.sum(squares[:, COLS:], axis=1)])
    weight_squares = jnp.sum(weights * weights, axis=(1, 2))
    payload = jnp.concatenate([col_part, jnp.sum(row_moments, axis=1), weight_squares, jnp.zeros((124,), F32)])
    dp_sums = jnp.sum(spread(payload.reshape(1, 6, 128), DP, N_DP).reshape(N_DP, 768), axis=0)
    col_sum = dp_sums[: 2 * COLS].reshape(2, COLS)
    moments_total = dp_sums[2 * COLS : 2 * COLS + 2]
    totals = jnp.concatenate([jnp.sum(col_sum, axis=1), dp_sums[2 * COLS + 2 : 2 * COLS + 4]])
    payload = jnp.concatenate([row_part.reshape(128), totals, jnp.zeros((124,), F32)])
    mp_sums = jnp.sum(spread(payload.reshape(1, 2, 128), MP, N_MP).reshape(N_MP, 256), axis=0)
    row_sum = mp_sums[:128].reshape(2, ROWS)
    squares_total = mp_sums[128:130]
    weight_total = mp_sums[130:132]
    new_rows = 0.5 * row_moments + 0.5 * (row_sum / FF)
    new_cols = 0.5 * col_moments + 0.5 * (col_sum / D)
    row_level = 0.5 * (moments_total / D) + 0.5 * (squares_total / (FF * D))
    step_scale = jnp.sqrt(weight_total / (D * FF))
    estimate = new_rows[:, :, None] * new_cols[:, None, :] / row_level[:, None, None]
    own = jnp.stack([own[:, :COLS], own[:, COLS:]])
    weight_step = step_scale[:, None, None] * (own * lax.rsqrt(estimate))
    return (input_grad, weight_step, new_rows, new_cols)


def solution(mesh):
    fine = Mesh(mesh.devices.reshape(N_YLO, N_Z, N_X, N_YHI, N_CORE), DP + MP)
    return jax.shard_map(
        shards,
        mesh=fine,
        in_specs=(P(DP, MP), P(DP, MP), P(None, DP, MP), P(None, DP), P(None, MP)),
        out_specs=(P(DP, MP), P(None, DP, MP), P(None, DP), P(None, MP)),
        check_vma=False,
    )
```

```python
import functools
import jax
import jax.numpy as jnp
from jax import lax
from jax.experimental import pallas as pl
from jax.experimental.pallas import tpu as pltpu
from jax.sharding import Mesh, PartitionSpec as P

D = 2048
FF = 5120
N_YLO, N_Z, N_X, N_YHI, N_CORE = 4, 8, 4, 2, 2
N_DP = N_YLO * N_Z
N_MP = N_X * N_YHI * N_CORE
N_XY = N_X * N_YHI
TOK = 368
ROWS = D // N_DP
COLS = FF // N_MP
FEAT = D // N_MP
SCALING = D ** (-0.5)
DP = ("ylo", "z")
XY = ("x", "yhi")
MP = ("x", "yhi", "core")
F32 = jnp.float32
BF16 = jnp.bfloat16


def gelu_parts(values):
    cubed_values = values * values * values
    argument = 0.7978845608 * (values + 0.044715 * cubed_values)
    tangent = jnp.tanh(argument)
    gelu_value = 0.5 * values * (1.0 + tangent)
    gelu_slope = 0.5 * (1.0 + tangent) + 0.5 * values * (1.0 - tangent * tangent) * 0.7978845608 * (
        1.0 + 3.0 * 0.044715 * values * values
    )
    return (gelu_value, gelu_slope)


def weight_block(w_ref, s):
    ylo, z = s // 4, 2 * (s % 4)
    return jnp.concatenate([w_ref[z, ylo], w_ref[z + 1, ylo]], axis=0)


def block_views(ref, s):
    return ref.at[pl.ds(2 * (s % 4), 4), s // 4]


def grads_kernel(tok_ref, w_hbm, cot_ref, grads_hbm, hidden_ref, w_ref, grads_ref, in_sem, out_sem):
    pairs = N_MP // 2
    loads = [
        pltpu.make_async_copy(block_views(w_hbm, 2 * p), w_ref.at[p], in_sem.at[p]) for p in range(pairs)
    ]
    stores = [
        pltpu.make_async_copy(grads_ref.at[p], block_views(grads_hbm, 2 * p), out_sem.at[p]) for p in range(pairs)
    ]
    for load in loads:
        load.start()
    acc = jnp.zeros((TOK, 2 * COLS), F32)
    for p in range(pairs):
        loads[p].wait()
        left = jnp.concatenate([tok_ref[0, p], tok_ref[1, p]], axis=1)
        right = w_ref[p].reshape(4 * ROWS, 2 * COLS)
        acc = acc + jnp.dot(left, right, preferred_element_type=F32)
    acc = acc * SCALING
    gelu_value, gelu_slope = gelu_parts(acc[:, :COLS])
    cot = cot_ref[...].astype(F32)
    hidden_ref[:, :COLS] = (cot * acc[:, COLS:] * gelu_slope).astype(BF16)
    hidden_ref[:, COLS:] = (cot * gelu_value).astype(BF16)
    hidden = hidden_ref[...]
    for p in range(pairs):
        left = jnp.concatenate([tok_ref[0, p], tok_ref[1, p]], axis=1)
        product = lax.dot_general(left, hidden, (((0,), (0,)), ((), ())), preferred_element_type=F32)
        grads_ref[p] = (product * SCALING).astype(BF16).reshape(4, ROWS, 2 * COLS)
        stores[p].start()
    for store in stores:
        store.wait()


def input_kernel(hidden_ref, w_ref, out_ref):
    hidden = hidden_ref[...]
    for s in range(0, N_MP, 2):
        right = jnp.concatenate([weight_block(w_ref, s), weight_block(w_ref, s + 1)], axis=0)
        product = lax.dot_general(hidden, right, (((1,), (1,)), ((), ())), preferred_element_type=F32)
        product = (product * SCALING).astype(BF16)
        out_ref[0, s // 2] = product[:, :FEAT]
        out_ref[1, s // 2] = product[:, FEAT:]


def call(kernel, out_shape, flops, in_specs, out_specs, scratch, *args):
    return pl.pallas_call(
        kernel,
        out_shape=out_shape,
        in_specs=in_specs,
        out_specs=out_specs,
        scratch_shapes=scratch,
        compiler_params=pltpu.CompilerParams(vmem_limit_bytes=40 * 2**20),
        cost_estimate=pl.CostEstimate(flops=flops, bytes_accessed=8 * 2**20, transcendentals=0),
    )(*args)


def spread(values, axis, size):
    return lax.all_to_all(jnp.broadcast_to(values[None], (size,) + values.shape), axis, 0, 0, tiled=True)


def shards(tokens, cotangent, weights, row_moments, col_moments):
    barrier = lax.optimization_barrier
    half = weights.astype(BF16)
    half = jnp.concatenate([half[0], half[1]], axis=1)
    some_rows = spread(half, "ylo", N_YLO)
    some_rows, tokens = barrier((some_rows, tokens))
    full = lax.all_gather(some_rows, "z", axis=0)
    features = spread(spread(tokens, XY, N_XY), "core", N_CORE)
    weight_squares = jnp.sum(weights * weights, axis=(1, 2))
    moments_sums = jnp.sum(row_moments, axis=1)

    flops = 2 * TOK * D * 2 * COLS
    vmem = pl.BlockSpec(memory_space=pltpu.VMEM)
    hbm = pl.BlockSpec(memory_space=pl.ANY)
    pairs = N_MP // 2
    grads, hidden = call(
        grads_kernel,
        [jax.ShapeDtypeStruct((N_Z, N_YLO, ROWS, 2 * COLS), BF16), jax.ShapeDtypeStruct((TOK, 2 * COLS), BF16)],
        2 * flops,
        [vmem, hbm, vmem],
        [hbm, vmem],
        [
            pltpu.VMEM((pairs, 4, ROWS, 2 * COLS), BF16),
            pltpu.VMEM((pairs, 4, ROWS, 2 * COLS), BF16),
            pltpu.SemaphoreType.DMA((pairs,)),
            pltpu.SemaphoreType.DMA((pairs,)),
        ],
        features, full, cotangent,
    )
    some_grads = lax.psum_scatter(grads, "z", scatter_dimension=0, tiled=False)
    terms = call(
        input_kernel,
        jax.ShapeDtypeStruct((N_CORE, N_XY, TOK, FEAT), BF16),
        flops, [vmem, vmem], vmem, [], hidden, full,
    )
    terms = lax.all_to_all(terms, "core", 0, 0, tiled=True)
    terms = (terms[0].astype(F32) + terms[1].astype(F32)).astype(BF16)
    terms = lax.all_to_all(terms, XY, 0, 0, tiled=True)
    input_grad = jnp.sum(terms.astype(F32), axis=0).astype(BF16)

    some_grads, input_grad = barrier((some_grads, input_grad))
    own = jnp.sum(lax.all_to_all(some_grads, "ylo", 0, 0, tiled=True).astype(F32), axis=0)
    squares = own * own + 1e-30
    col_part = jnp.sum(squares, axis=0)
    row_part = jnp.stack([jnp.sum(squares[:, :COLS], axis=1), jnp.sum(squares[:, COLS:], axis=1)]).reshape(128)
    payload = jnp.concatenate([col_part, moments_sums, weight_squares, jnp.zeros((124,), F32)]).reshape(1, 6, 128)
    payload = jnp.broadcast_to(payload, (N_DP, 6, 128))
    payload, row_part, own = barrier((payload, row_part, own))
    dp_sums = jnp.sum(lax.all_to_all(payload, DP, 0, 0, tiled=True), axis=0).reshape(768)
    col_sum = dp_sums[: 2 * COLS].reshape(2, COLS)
    new_cols = 0.5 * col_moments + 0.5 * (col_sum / D)
    moments_total = dp_sums[2 * COLS : 2 * COLS + 2]
    totals = jnp.concatenate([jnp.sum(col_sum, axis=1), dp_sums[2 * COLS + 2 : 2 * COLS + 4]])
    payload = jnp.concatenate([row_part, totals, jnp.zeros((124,), F32)]).reshape(1, 2, 128)
    payload = jnp.broadcast_to(payload, (N_MP, 2, 128))
    payload, new_cols, moments_total, own = barrier((payload, new_cols, moments_total, own))
    mp_sums = jnp.sum(lax.all_to_all(payload, MP, 0, 0, tiled=True), axis=0).reshape(256)
    row_sum = mp_sums[:128].reshape(2, ROWS)
    squares_total = mp_sums[128:130]
    weight_total = mp_sums[130:132]
    new_rows = 0.5 * row_moments + 0.5 * (row_sum / FF)
    row_level = 0.5 * (moments_total / D) + 0.5 * (squares_total / (FF * D))
    step_scale = jnp.sqrt(weight_total / (D * FF))
    estimate = new_rows[:, :, None] * new_cols[:, None, :] / row_level[:, None, None]
    own = jnp.stack([own[:, :COLS], own[:, COLS:]])
    weight_step = step_scale[:, None, None] * (own * lax.rsqrt(estimate))
    return (input_grad, weight_step, new_rows, new_cols)


def solution(mesh):
    fine = Mesh(mesh.devices.reshape(N_YLO, N_Z, N_X, N_YHI, N_CORE), DP + MP)
    return jax.shard_map(
        shards,
        mesh=fine,
        in_specs=(P(DP, MP), P(DP, MP), P(None, DP, MP), P(None, DP), P(None, MP)),
        out_specs=(P(DP, MP), P(None, DP, MP), P(None, DP), P(None, MP)),
        check_vma=False,
    )
```

```python
import functools
import jax
import jax.numpy as jnp
from jax import lax
from jax.experimental import pallas as pl
from jax.experimental.pallas import tpu as pltpu
from jax.sharding import Mesh, PartitionSpec as P

D = 2048
FF = 5120
N_YH, N_YL, N_Z, N_X, N_YHI, N_CORE = 2, 2, 8, 4, 2, 2
N_DP = N_YH * N_YL * N_Z
N_MP = N_X * N_YHI * N_CORE
N_GROUP = N_YH * N_Z
TOK = 368
ROWS = D // N_DP
COLS = FF // N_MP
FEAT = D // N_MP
SCALING = D ** (-0.5)
DP = ("yh", "yl", "z")
MP = ("x", "yhi", "core")
GROUP = ("yh", "z")
PLANE = ("yl", "x", "yhi")
F32 = jnp.float32
BF16 = jnp.bfloat16


def gelu_parts(values):
    cubed_values = values * values * values
    argument = 0.7978845608 * (values + 0.044715 * cubed_values)
    tangent = jnp.tanh(argument)
    gelu_value = 0.5 * values * (1.0 + tangent)
    gelu_slope = 0.5 * (1.0 + tangent) + 0.5 * values * (1.0 - tangent * tangent) * 0.7978845608 * (
        1.0 + 3.0 * 0.044715 * values * values
    )
    return (gelu_value, gelu_slope)


def token_pair(own_ref, other_ref, place_ref, group, i, j):
    d = (place_ref[0] + group) % 2 + 2 * i
    mine, other = own_ref[d, j], other_ref[d, j]
    return jnp.concatenate([mine, other], axis=1)


def weight_places(place_ref, group, i, j, sign):
    d = (place_ref[0] + group) % 2 + 2 * i
    row = ((place_ref[1] + sign * d + 4) % 4) // 2
    high = (place_ref[2] + j) % 2
    return row, 2 * high + place_ref[3], 2 * high + (place_ref[3] + 1) % 2


def weight_pair(w_ref, place_ref, group, i, j, sign):
    row, first, second = weight_places(place_ref, group, i, j, sign)
    return jnp.concatenate([w_ref[at, low, row] for at in (first, second) for low in range(2)], axis=0)


def product_kernel(group, place_ref, own_ref, other_ref, w_ref, out_ref):
    acc = None
    for i in range(2):
        for j in range(2):
            term = jnp.dot(
                token_pair(own_ref, other_ref, place_ref, group, i, j),
                weight_pair(w_ref, place_ref, group, i, j, -1),
                preferred_element_type=F32,
            )
            acc = term if acc is None else acc + term
    out_ref[...] = acc.astype(out_ref.dtype)


def hidden_kernel(mine_ref, cot_ref, received_any, hidden_ref, received_ref, sem):
    load = pltpu.make_async_copy(received_any, received_ref, sem)
    load.start()
    cot = cot_ref[...].astype(F32)
    load.wait()
    total = (mine_ref[...] + received_ref[...].astype(F32)) * SCALING
    gelu_value, gelu_slope = gelu_parts(total[:, :COLS])
    hidden_ref[:, :COLS] = (cot * total[:, COLS:] * gelu_slope).astype(BF16)
    hidden_ref[:, COLS:] = (cot * gelu_value).astype(BF16)


def grads_kernel(place_ref, own_ref, other_ref, hidden_ref, out_ref):
    hidden = hidden_ref[...]
    for i in range(2):
        for j in range(2):
            left = token_pair(own_ref, other_ref, place_ref, 0, i, j)
            product = lax.dot_general(left, hidden, (((0,), (0,)), ((), ())), preferred_element_type=F32)
            out_ref[i, j] = product


def grads_sum_kernel(place_ref, own_ref, other_ref, hidden_ref, mine_ref, out_ref):
    hidden = hidden_ref[...]
    for i in range(2):
        for j in range(2):
            left = token_pair(own_ref, other_ref, place_ref, 1, i, j)
            product = lax.dot_general(left, hidden, (((0,), (0,)), ((), ())), preferred_element_type=F32)
            row, first, second = weight_places(place_ref, 1, i, j, -1)
            mine_row = weight_places(place_ref, 0, 0, j, -1)[0]
            product = product + mine_ref[(mine_row + row) % 2, j]
            product = (product * SCALING).astype(BF16)
            out_ref[row, first] = product[:FEAT]
            out_ref[row, second] = product[FEAT:]


def input_kernel(place_ref, mine_ref, pair_ref, w_ref, own_ref, other_ref):
    for group in range(2):
        hidden = (pair_ref if group else mine_ref)[...]
        for i in range(2):
            for j in range(2):
                right = weight_pair(w_ref, place_ref, group, i, j, 1)
                product = lax.dot_general(hidden, right, (((1,), (1,)), ((), ())), preferred_element_type=F32)
                product = (product * SCALING).astype(BF16)
                e = (place_ref[0] + group) % 2 + 2 * i
                own_ref[e, j] = product[:, :FEAT]
                other_ref[e, j] = product[:, FEAT:]


def squares_kernel(parts_ref, stats_ref, own_ref, payload_ref, rows_ref):
    own = parts_ref[0].astype(F32)
    for part in range(1, N_GROUP):
        own = own + parts_ref[part].astype(F32)
    own_ref[...] = own
    squares = own * own + 1e-30
    cols = jnp.sum(squares, axis=0, keepdims=True)
    lines = [cols[:, 128 * i : 128 * (i + 1)] for i in range(5)]
    block = jnp.concatenate(lines + [stats_ref[...], jnp.zeros((2, 128), F32)], axis=0)
    payload_ref[...] = jnp.broadcast_to(block[None], payload_ref.shape)
    ones = jnp.ones((8, COLS), F32)
    for k in range(2):
        rows_ref[:, k * ROWS : (k + 1) * ROWS] = lax.dot_general(
            ones,
            squares[:, k * COLS : (k + 1) * COLS],
            (((1,), (1,)), ((), ())),
            precision=lax.Precision.HIGHEST,
            preferred_element_type=F32,
        )


def columns_kernel(received_ref, rows_ref, col_moments_ref, payload_ref, new_cols_ref, kept_ref, cols_ref):
    total = jnp.sum(received_ref[...], axis=0)
    cols = jnp.concatenate([total[i : i + 1] for i in range(5)], axis=1)
    kept = total[5:6]
    kept_ref[...] = kept
    lane = lax.broadcasted_iota(jnp.int32, (1, 128), 1)
    line = kept
    for k in range(2):
        part = cols[:, k * COLS : (k + 1) * COLS]
        new_cols = 0.5 * col_moments_ref[k : k + 1] + 0.5 * (part / D)
        new_cols_ref[k : k + 1] = new_cols
        cols_ref[k : k + 1] = new_cols
        line = jnp.where(lane == k, jnp.sum(part, axis=1, keepdims=True), line)
    block = jnp.concatenate([rows_ref[0:1], line, jnp.zeros((6, 128), F32)], axis=0)
    payload_ref[...] = jnp.broadcast_to(block[None], payload_ref.shape)


def step_kernel(received_ref, own_ref, kept_ref, half_moments_ref, new_cols_ref, step_ref, new_rows_ref):
    total = jnp.sum(received_ref[...], axis=0)
    diagonal = lax.broadcasted_iota(jnp.int32, (ROWS, ROWS), 0) == lax.broadcasted_iota(jnp.int32, (ROWS, ROWS), 1)
    for k in range(2):
        row_sum = total[0:1, k * ROWS : (k + 1) * ROWS]
        new_rows = half_moments_ref[k : k + 1] + 0.5 * (row_sum / FF)
        new_rows_ref[k : k + 1] = new_rows
        upright = jnp.sum(jnp.where(diagonal, new_rows, 0.0), axis=1, keepdims=True)
        row_level = 0.5 * (kept_ref[0:1, k : k + 1] / D) + 0.5 * (total[1:2, k : k + 1] / (FF * D))
        step_scale = jnp.sqrt(total[1:2, 2 + k : 3 + k] / (D * FF))
        estimate = upright * new_cols_ref[k : k + 1] / row_level
        step_ref[k] = step_scale * (own_ref[:, k * COLS : (k + 1) * COLS] * lax.rsqrt(estimate))


def call(kernel, out_shape, flops, *args, scratch=(), late=False):
    vmem = pl.BlockSpec(memory_space=pltpu.VMEM)
    smem = pl.BlockSpec(memory_space=pltpu.SMEM)
    specs = [smem if arg.dtype == jnp.int32 else vmem for arg in args]
    if late:
        specs[-1] = pl.BlockSpec(memory_space=pl.ANY)
    return pl.pallas_call(
        kernel,
        out_shape=out_shape,
        in_specs=specs,
        out_specs=jax.tree.map(lambda _: vmem, out_shape),
        scratch_shapes=scratch,
        compiler_params=pltpu.CompilerParams(vmem_limit_bytes=12 * 2**20),
        cost_estimate=pl.CostEstimate(flops=flops, bytes_accessed=4 * 2**20, transcendentals=0),
    )(*args)


def struct(shape, dtype=F32):
    return jax.ShapeDtypeStruct(shape, dtype)


def spread(values, axis, size):
    return lax.all_to_all(jnp.broadcast_to(values[None], (size,) + values.shape), axis, 0, 0, tiled=True)


def home_pairs(flip):
    pairs = []
    for yl in range(N_YL):
        for x in range(N_X):
            for yhi in range(N_YHI):
                swap = (yl + x) % 2
                target = ((yl ^ swap) * N_X + (x ^ swap)) * N_YHI + (yhi ^ flip)
                pairs.append(((yl * N_X + x) * N_YHI + yhi, target))
    return pairs


def x_shift(values, step):
    return lax.ppermute(values, "x", [(i, (i + step) % N_X) for i in range(N_X)])


def exchange(values, axis):
    return lax.ppermute(values, axis, [(0, 1), (1, 0)])


def shards(tokens, cotangent, weights, row_moments, col_moments):
    barrier = lax.optimization_barrier
    x, yhi, core, half_index = (lax.axis_index(name) for name in ("x", "yhi", "core", "yl"))
    place = jnp.stack([(x + half_index) % 2, x, yhi, core]).astype(jnp.int32)
    near = lax.ppermute(tokens, PLANE, home_pairs(0))
    far = lax.ppermute(tokens, PLANE, home_pairs(1))
    half = weights.astype(BF16)
    half = jnp.concatenate([half[0], half[1]], axis=1)
    pair_half = exchange(half, "yh")
    first = lax.axis_index("yh") == 0
    both = jnp.stack([jnp.where(first, half, pair_half), jnp.where(first, pair_half, half)])
    both, near = barrier((both, near))
    full = spread(both, "z", N_Z).reshape(N_Z // 2, 2, N_YH, ROWS, 2 * COLS)
    blocks = jnp.stack([near, far])
    blocks = jnp.stack([blocks] + [x_shift(blocks, step) for step in range(1, N_X)])
    others = exchange(blocks, "core")
    weight_squares = jnp.sum(weights * weights, axis=(1, 2))
    stats = jnp.concatenate([jnp.sum(row_moments, axis=1), weight_squares, jnp.zeros((124,), F32)]).reshape(1, 128)

    flops = 2 * TOK * (D // 2) * 2 * COLS
    wide = (TOK, 2 * COLS)
    grads_shape = (N_YH, N_X, 2 * ROWS, 2 * COLS)
    for_pair = call(functools.partial(product_kernel, 1), struct(wide, BF16), flops, place, blocks, others, full)
    mine = call(functools.partial(product_kernel, 0), struct(wide), flops, place, blocks, others, full)
    hidden = call(
        hidden_kernel, struct(wide, BF16), 10**7, mine, cotangent, exchange(for_pair, "yl"),
        scratch=[pltpu.VMEM(wide, BF16), pltpu.SemaphoreType.DMA],
        late=True,
    )
    pair_hidden = exchange(hidden, "yl")
    grads = call(grads_kernel, struct((2, 2, 2 * FEAT, 2 * COLS)), flops, place, blocks, others, hidden)
    grads = call(
        grads_sum_kernel, struct(grads_shape, BF16), flops, place, blocks, others, pair_hidden, grads
    )
    parts = lax.all_to_all(grads.reshape(N_GROUP, ROWS, 2 * COLS), GROUP, 0, 0, tiled=True)

    shape = struct((N_X, N_YHI, TOK, FEAT), BF16)
    terms, others = call(input_kernel, [shape, shape], 2 * flops, place, hidden, pair_hidden, full)
    terms = (terms.astype(F32) + exchange(others, "core").astype(F32)).astype(BF16)
    total = terms[0].astype(F32)
    for step in range(1, N_X):
        total = total + x_shift(terms[step], step).astype(F32)
    total = total.astype(BF16)
    near = lax.ppermute(total[0], PLANE, home_pairs(0))
    far = lax.ppermute(total[1], PLANE, home_pairs(1))
    input_grad = (near.astype(F32) + far.astype(F32)).astype(BF16)

    stats, half_moments, hidden = barrier((stats, 0.5 * row_moments, hidden))
    own, payload, rows = call(
        squares_kernel, [struct((ROWS, 2 * COLS)), struct((N_DP, 8, 128)), struct((8, 128))], 10**6, parts, stats
    )
    received = lax.all_to_all(payload, DP, 0, 0, tiled=True)
    payload, new_cols, kept, cols = call(
        columns_kernel,
        [struct((N_MP, 8, 128)), struct((2, COLS)), struct((1, 128)), struct((2, COLS))],
        10**6, received, rows, col_moments,
    )
    received = lax.all_to_all(payload, MP, 0, 0, tiled=True)
    weight_step, new_rows = call(
        step_kernel, [struct((2, ROWS, COLS)), struct((2, ROWS))], 10**6, received, own, kept, half_moments, cols
    )
    return (input_grad, weight_step, new_rows, new_cols)


def solution(mesh):
    fine = Mesh(mesh.devices.reshape(N_YH, N_YL, N_Z, N_X, N_YHI, N_CORE), DP + MP)
    return jax.shard_map(
        shards,
        mesh=fine,
        in_specs=(P(DP, MP), P(DP, MP), P(None, DP, MP), P(None, DP), P(None, MP)),
        out_specs=(P(DP, MP), P(None, DP, MP), P(None, DP), P(None, MP)),
        check_vma=False,
    )
```

```python
import functools
import jax
import jax.numpy as jnp
from jax import lax
from jax.experimental import pallas as pl
from jax.experimental.pallas import tpu as pltpu
from jax.sharding import Mesh, PartitionSpec as P

D = 2048
FF = 5120
N_YH, N_YL, N_Z, N_X, N_YHI, N_CORE = 2, 2, 8, 4, 2, 2
N_DP = N_YH * N_YL * N_Z
N_MP = N_X * N_YHI * N_CORE
N_GROUP = N_YH * N_Z
TOK = 368
ROWS = D // N_DP
COLS = FF // N_MP
FEAT = D // N_MP
SCALING = D ** (-0.5)
DP = ("yh", "yl", "z")
MP = ("x", "yhi", "core")
GROUP = ("yh", "z")
PLANE = ("yl", "x", "yhi")
F32 = jnp.float32
BF16 = jnp.bfloat16


def gelu_parts(values):
    cubed_values = values * values * values
    argument = 0.7978845608 * (values + 0.044715 * cubed_values)
    tangent = jnp.tanh(argument)
    gelu_value = 0.5 * values * (1.0 + tangent)
    gelu_slope = 0.5 * (1.0 + tangent) + 0.5 * values * (1.0 - tangent * tangent) * 0.7978845608 * (
        1.0 + 3.0 * 0.044715 * values * values
    )
    return (gelu_value, gelu_slope)


def token_pair(own_ref, other_ref, place_ref, group, i, j):
    d = (place_ref[0] + group) % 2 + 2 * i
    mine, other = own_ref[d, j], other_ref[d, j]
    return jnp.concatenate([mine, other], axis=1)


def weight_places(place_ref, group, i, j, sign):
    d = (place_ref[0] + group) % 2 + 2 * i
    row = ((place_ref[1] + sign * d + 4) % 4) // 2
    high = (place_ref[2] + j) % 2
    return row, 2 * high + place_ref[3], 2 * high + (place_ref[3] + 1) % 2


def weight_pair(w_ref, place_ref, group, i, j, sign):
    row, first, second = weight_places(place_ref, group, i, j, sign)
    return jnp.concatenate([w_ref[at, low, row] for at in (first, second) for low in range(2)], axis=0)


def product_kernel(group, place_ref, own_ref, other_ref, w_ref, out_ref):
    acc = None
    for i in range(2):
        for j in range(2):
            term = jnp.dot(
                token_pair(own_ref, other_ref, place_ref, group, i, j),
                weight_pair(w_ref, place_ref, group, i, j, -1),
                preferred_element_type=F32,
            )
            acc = term if acc is None else acc + term
    out_ref[...] = acc.astype(out_ref.dtype)


def hidden_kernel(mine_ref, cot_ref, received_any, hidden_ref, received_ref, sem):
    load = pltpu.make_async_copy(received_any, received_ref, sem)
    load.start()
    cot = cot_ref[...].astype(F32)
    load.wait()
    total = (mine_ref[...] + received_ref[...].astype(F32)) * SCALING
    gelu_value, gelu_slope = gelu_parts(total[:, :COLS])
    hidden_ref[:, :COLS] = (cot * total[:, COLS:] * gelu_slope).astype(BF16)
    hidden_ref[:, COLS:] = (cot * gelu_value).astype(BF16)


def grads_kernel(place_ref, own_ref, other_ref, hidden_ref, out_ref):
    hidden = hidden_ref[...]
    for i in range(2):
        for j in range(2):
            left = token_pair(own_ref, other_ref, place_ref, 0, i, j)
            product = lax.dot_general(left, hidden, (((0,), (0,)), ((), ())), preferred_element_type=F32)
            out_ref[i, j] = product


def grads_sum_kernel(place_ref, own_ref, other_ref, hidden_ref, mine_ref, out_ref):
    hidden = hidden_ref[...]
    for i in range(2):
        for j in range(2):
            left = token_pair(own_ref, other_ref, place_ref, 1, i, j)
            product = lax.dot_general(left, hidden, (((0,), (0,)), ((), ())), preferred_element_type=F32)
            row, first, second = weight_places(place_ref, 1, i, j, -1)
            mine_row = weight_places(place_ref, 0, 0, j, -1)[0]
            product = product + mine_ref[(mine_row + row) % 2, j]
            product = (product * SCALING).astype(BF16)
            out_ref[row, first] = product[:FEAT]
            out_ref[row, second] = product[FEAT:]


def input_kernel(place_ref, mine_ref, pair_ref, w_ref, own_ref, other_ref):
    for group in range(2):
        hidden = (pair_ref if group else mine_ref)[...]
        for i in range(2):
            for j in range(2):
                right = weight_pair(w_ref, place_ref, group, i, j, 1)
                product = lax.dot_general(hidden, right, (((1,), (1,)), ((), ())), preferred_element_type=F32)
                product = (product * SCALING).astype(BF16)
                e = (place_ref[0] + group) % 2 + 2 * i
                own_ref[e, j] = product[:, :FEAT]
                other_ref[e, j] = product[:, FEAT:]


def squares_kernel(parts_ref, stats_ref, own_ref, payload_ref, rows_ref):
    own = parts_ref[0].astype(F32)
    for part in range(1, N_GROUP):
        own = own + parts_ref[part].astype(F32)
    own_ref[...] = own
    squares = own * own + 1e-30
    cols = jnp.sum(squares, axis=0, keepdims=True)
    lines = [cols[:, 128 * i : 128 * (i + 1)] for i in range(5)]
    block = jnp.concatenate(lines + [stats_ref[...], jnp.zeros((2, 128), F32)], axis=0)
    payload_ref[...] = jnp.broadcast_to(block[None], payload_ref.shape)
    ones = jnp.ones((8, COLS), F32)
    for k in range(2):
        rows_ref[:, k * ROWS : (k + 1) * ROWS] = lax.dot_general(
            ones,
            squares[:, k * COLS : (k + 1) * COLS],
            (((1,), (1,)), ((), ())),
            precision=lax.Precision.HIGHEST,
            preferred_element_type=F32,
        )


def columns_kernel(received_ref, rows_ref, col_moments_ref, payload_ref, new_cols_ref, kept_ref, cols_ref):
    total = jnp.sum(received_ref[...], axis=0)
    cols = jnp.concatenate([total[i : i + 1] for i in range(5)], axis=1)
    kept = total[5:6]
    kept_ref[...] = kept
    lane = lax.broadcasted_iota(jnp.int32, (1, 128), 1)
    line = kept
    for k in range(2):
        part = cols[:, k * COLS : (k + 1) * COLS]
        new_cols = 0.5 * col_moments_ref[k : k + 1] + 0.5 * (part / D)
        new_cols_ref[k : k + 1] = new_cols
        cols_ref[k : k + 1] = new_cols
        line = jnp.where(lane == k, jnp.sum(part, axis=1, keepdims=True), line)
    block = jnp.concatenate([rows_ref[0:1], line, jnp.zeros((6, 128), F32)], axis=0)
    payload_ref[...] = jnp.broadcast_to(block[None], payload_ref.shape)


def step_kernel(received_ref, own_ref, kept_ref, half_moments_ref, new_cols_ref, step_ref, new_rows_ref):
    total = jnp.sum(received_ref[...], axis=0)
    diagonal = lax.broadcasted_iota(jnp.int32, (ROWS, ROWS), 0) == lax.broadcasted_iota(jnp.int32, (ROWS, ROWS), 1)
    for k in range(2):
        row_sum = total[0:1, k * ROWS : (k + 1) * ROWS]
        new_rows = half_moments_ref[k : k + 1] + 0.5 * (row_sum / FF)
        new_rows_ref[k : k + 1] = new_rows
        upright = jnp.sum(jnp.where(diagonal, new_rows, 0.0), axis=1, keepdims=True)
        row_level = 0.5 * (kept_ref[0:1, k : k + 1] / D) + 0.5 * (total[1:2, k : k + 1] / (FF * D))
        step_scale = jnp.sqrt(total[1:2, 2 + k : 3 + k] / (D * FF))
        estimate = upright * new_cols_ref[k : k + 1] / row_level
        step_ref[k] = step_scale * (own_ref[:, k * COLS : (k + 1) * COLS] * lax.rsqrt(estimate))


def call(kernel, out_shape, flops, *args, scratch=(), late=False):
    vmem = pl.BlockSpec(memory_space=pltpu.VMEM)
    smem = pl.BlockSpec(memory_space=pltpu.SMEM)
    specs = [smem if arg.dtype == jnp.int32 else vmem for arg in args]
    if late:
        specs[-1] = pl.BlockSpec(memory_space=pl.ANY)
    return pl.pallas_call(
        kernel,
        out_shape=out_shape,
        in_specs=specs,
        out_specs=jax.tree.map(lambda _: vmem, out_shape),
        scratch_shapes=scratch,
        compiler_params=pltpu.CompilerParams(vmem_limit_bytes=12 * 2**20),
        cost_estimate=pl.CostEstimate(flops=flops, bytes_accessed=4 * 2**20, transcendentals=0),
    )(*args)


def struct(shape, dtype=F32):
    return jax.ShapeDtypeStruct(shape, dtype)


def spread(values, axis, size):
    return lax.all_to_all(jnp.broadcast_to(values[None], (size,) + values.shape), axis, 0, 0, tiled=True)


def home_pairs(flip):
    pairs = []
    for yl in range(N_YL):
        for x in range(N_X):
            for yhi in range(N_YHI):
                swap = (yl + x) % 2
                target = ((yl ^ swap) * N_X + (x ^ swap)) * N_YHI + (yhi ^ flip)
                pairs.append(((yl * N_X + x) * N_YHI + yhi, target))
    return pairs


def x_shift(values, step):
    return lax.ppermute(values, "x", [(i, (i + step) % N_X) for i in range(N_X)])


def exchange(values, axis):
    return lax.ppermute(values, axis, [(0, 1), (1, 0)])


def shards(tokens, cotangent, weights, row_moments, col_moments):
    barrier = lax.optimization_barrier
    x, yhi, core, half_index = (lax.axis_index(name) for name in ("x", "yhi", "core", "yl"))
    place = jnp.stack([(x + half_index) % 2, x, yhi, core]).astype(jnp.int32)
    near = lax.ppermute(tokens, PLANE, home_pairs(0))
    far = lax.ppermute(tokens, PLANE, home_pairs(1))
    half = weights.astype(BF16)
    half = jnp.concatenate([half[0], half[1]], axis=1)
    pair_half = exchange(half, "yh")
    first = lax.axis_index("yh") == 0
    both = jnp.stack([jnp.where(first, half, pair_half), jnp.where(first, pair_half, half)])
    both, near = barrier((both, near))
    full = spread(both, "z", N_Z).reshape(N_Z // 2, 2, N_YH, ROWS, 2 * COLS)
    blocks = jnp.stack([near, far])
    blocks = jnp.stack([blocks] + [x_shift(blocks, step) for step in range(1, N_X)])
    others = exchange(blocks, "core")
    weight_squares = jnp.sum(weights * weights, axis=(1, 2))
    stats = jnp.concatenate([jnp.sum(row_moments, axis=1), weight_squares, jnp.zeros((124,), F32)]).reshape(1, 128)

    flops = 2 * TOK * (D // 2) * 2 * COLS
    wide = (TOK, 2 * COLS)
    grads_shape = (N_YH, N_X, 2 * ROWS, 2 * COLS)
    for_pair = call(functools.partial(product_kernel, 1), struct(wide, BF16), flops, place, blocks, others, full)
    mine = call(functools.partial(product_kernel, 0), struct(wide), flops, place, blocks, others, full)
    summed = (mine + exchange(for_pair, "yl").astype(F32)) * SCALING
    gelu_value, gelu_slope = gelu_parts(summed[:, :COLS])
    hidden = jnp.concatenate(
        [
            (cotangent.astype(F32) * summed[:, COLS:] * gelu_slope).astype(BF16),
            (cotangent.astype(F32) * gelu_value).astype(BF16),
        ],
        axis=1,
    )
    pair_hidden = exchange(hidden, "yl")
    grads = call(grads_kernel, struct((2, 2, 2 * FEAT, 2 * COLS)), flops, place, blocks, others, hidden)
    grads = call(
        grads_sum_kernel, struct(grads_shape, BF16), flops, place, blocks, others, pair_hidden, grads
    )
    parts = lax.all_to_all(grads.reshape(N_GROUP, ROWS, 2 * COLS), GROUP, 0, 0, tiled=True)

    shape = struct((N_X, N_YHI, TOK, FEAT), BF16)
    terms, others = call(input_kernel, [shape, shape], 2 * flops, place, hidden, pair_hidden, full)
    terms = (terms.astype(F32) + exchange(others, "core").astype(F32)).astype(BF16)
    total = terms[0].astype(F32)
    for step in range(1, N_X):
        total = total + x_shift(terms[step], step).astype(F32)
    total = total.astype(BF16)
    near = lax.ppermute(total[0], PLANE, home_pairs(0))
    far = lax.ppermute(total[1], PLANE, home_pairs(1))
    parts, near = barrier((parts, near))
    input_grad = (near.astype(F32) + far.astype(F32)).astype(BF16)

    stats, half_moments, hidden = barrier((stats, 0.5 * row_moments, hidden))
    own, payload, rows = call(
        squares_kernel, [struct((ROWS, 2 * COLS)), struct((N_DP, 8, 128)), struct((8, 128))], 10**6, parts, stats
    )
    received = lax.all_to_all(payload, DP, 0, 0, tiled=True)
    payload, new_cols, kept, cols = call(
        columns_kernel,
        [struct((N_MP, 8, 128)), struct((2, COLS)), struct((1, 128)), struct((2, COLS))],
        10**6, received, rows, col_moments,
    )
    received = lax.all_to_all(payload, MP, 0, 0, tiled=True)
    weight_step, new_rows = call(
        step_kernel, [struct((2, ROWS, COLS)), struct((2, ROWS))], 10**6, received, own, kept, half_moments, cols
    )
    return (input_grad, weight_step, new_rows, new_cols)


def solution(mesh):
    fine = Mesh(mesh.devices.reshape(N_YH, N_YL, N_Z, N_X, N_YHI, N_CORE), DP + MP)
    return jax.shard_map(
        shards,
        mesh=fine,
        in_specs=(P(DP, MP), P(DP, MP), P(None, DP, MP), P(None, DP), P(None, MP)),
        out_specs=(P(DP, MP), P(None, DP, MP), P(None, DP), P(None, MP)),
        check_vma=False,
    )
```

```python
import functools
import jax
import jax.numpy as jnp
from jax import lax
from jax.experimental import pallas as pl
from jax.experimental.pallas import tpu as pltpu
from jax.sharding import Mesh, PartitionSpec as P

D = 2048
FF = 5120
N_YH, N_YL, N_Z, N_X, N_YHI, N_CORE = 2, 2, 8, 4, 2, 2
N_DP = N_YH * N_YL * N_Z
N_MP = N_X * N_YHI * N_CORE
N_GROUP = N_YH * N_Z
TOK = 368
ROWS = D // N_DP
COLS = FF // N_MP
FEAT = D // N_MP
SCALING = D ** (-0.5)
DP = ("yh", "yl", "z")
MP = ("x", "yhi", "core")
GROUP = ("yh", "z")
PLANE = ("yl", "x", "yhi")
F32 = jnp.float32
BF16 = jnp.bfloat16


def gelu_parts(values):
    cubed_values = values * values * values
    argument = 0.7978845608 * (values + 0.044715 * cubed_values)
    tangent = jnp.tanh(argument)
    gelu_value = 0.5 * values * (1.0 + tangent)
    gelu_slope = 0.5 * (1.0 + tangent) + 0.5 * values * (1.0 - tangent * tangent) * 0.7978845608 * (
        1.0 + 3.0 * 0.044715 * values * values
    )
    return (gelu_value, gelu_slope)


def token_pair(own_ref, other_ref, place_ref, group, i, j):
    d = (place_ref[0] + group) % 2 + 2 * i
    mine, other = own_ref[d, j], other_ref[d, j]
    return jnp.concatenate([mine, other], axis=1)


def weight_places(place_ref, group, i, j, sign):
    d = (place_ref[0] + group) % 2 + 2 * i
    row = ((place_ref[1] + sign * d + 4) % 4) // 2
    high = (place_ref[2] + j) % 2
    return row, 2 * high + place_ref[3], 2 * high + (place_ref[3] + 1) % 2


def weight_pair(w_ref, place_ref, group, i, j, sign):
    row, first, second = weight_places(place_ref, group, i, j, sign)
    return jnp.concatenate([w_ref[at, low, row] for at in (first, second) for low in range(2)], axis=0)


def product_kernel(group, place_ref, own_ref, other_ref, w_ref, out_ref):
    acc = None
    for i in range(2):
        for j in range(2):
            term = jnp.dot(
                token_pair(own_ref, other_ref, place_ref, group, i, j),
                weight_pair(w_ref, place_ref, group, i, j, -1),
                preferred_element_type=F32,
            )
            acc = term if acc is None else acc + term
    out_ref[...] = acc.astype(out_ref.dtype)


def hidden_kernel(mine_ref, cot_ref, received_any, hidden_ref, received_ref, sem):
    load = pltpu.make_async_copy(received_any, received_ref, sem)
    load.start()
    cot = cot_ref[...].astype(F32)
    load.wait()
    total = (mine_ref[...] + received_ref[...].astype(F32)) * SCALING
    gelu_value, gelu_slope = gelu_parts(total[:, :COLS])
    hidden_ref[:, :COLS] = (cot * total[:, COLS:] * gelu_slope).astype(BF16)
    hidden_ref[:, COLS:] = (cot * gelu_value).astype(BF16)


def grads_kernel(place_ref, own_ref, other_ref, hidden_ref, out_ref):
    hidden = hidden_ref[...]
    for i in range(2):
        for j in range(2):
            left = token_pair(own_ref, other_ref, place_ref, 0, i, j)
            product = lax.dot_general(left, hidden, (((0,), (0,)), ((), ())), preferred_element_type=F32)
            out_ref[i, j] = product


def grads_sum_kernel(place_ref, own_ref, other_ref, hidden_ref, mine_ref, out_ref):
    hidden = hidden_ref[...]
    for i in range(2):
        for j in range(2):
            left = token_pair(own_ref, other_ref, place_ref, 1, i, j)
            product = lax.dot_general(left, hidden, (((0,), (0,)), ((), ())), preferred_element_type=F32)
            row, first, second = weight_places(place_ref, 1, i, j, -1)
            mine_row = weight_places(place_ref, 0, 0, j, -1)[0]
            product = product + mine_ref[(mine_row + row) % 2, j]
            product = (product * SCALING).astype(BF16)
            for k in range(4):
                out_ref[second if k // 2 else first, k % 2, row] = product[k * ROWS : (k + 1) * ROWS]


def input_kernel(place_ref, mine_ref, pair_ref, w_ref, own_ref, other_ref):
    for group in range(2):
        hidden = (pair_ref if group else mine_ref)[...]
        for i in range(2):
            for j in range(2):
                right = weight_pair(w_ref, place_ref, group, i, j, 1)
                product = lax.dot_general(hidden, right, (((1,), (1,)), ((), ())), preferred_element_type=F32)
                product = (product * SCALING).astype(BF16)
                e = (place_ref[0] + group) % 2 + 2 * i
                own_ref[e, j] = product[:, :FEAT]
                other_ref[e, j] = product[:, FEAT:]


def squares_kernel(part_ref, received_ref, stats_ref, own_ref, payload_ref, rows_ref):
    own = part_ref[...] + received_ref[...].astype(F32)
    own_ref[...] = own
    squares = own * own + 1e-30
    cols = jnp.sum(squares, axis=0, keepdims=True)
    lines = [cols[:, 128 * i : 128 * (i + 1)] for i in range(5)]
    block = jnp.concatenate(lines + [stats_ref[...], jnp.zeros((2, 128), F32)], axis=0)
    payload_ref[...] = jnp.broadcast_to(block[None], payload_ref.shape)
    ones = jnp.ones((8, COLS), F32)
    for k in range(2):
        rows_ref[:, k * ROWS : (k + 1) * ROWS] = lax.dot_general(
            ones,
            squares[:, k * COLS : (k + 1) * COLS],
            (((1,), (1,)), ((), ())),
            precision=lax.Precision.HIGHEST,
            preferred_element_type=F32,
        )


def columns_kernel(received_ref, rows_ref, col_moments_ref, payload_ref, new_cols_ref, kept_ref, cols_ref):
    total = jnp.sum(received_ref[...], axis=0)
    cols = jnp.concatenate([total[i : i + 1] for i in range(5)], axis=1)
    kept = total[5:6]
    kept_ref[...] = kept
    lane = lax.broadcasted_iota(jnp.int32, (1, 128), 1)
    line = kept
    for k in range(2):
        part = cols[:, k * COLS : (k + 1) * COLS]
        new_cols = 0.5 * col_moments_ref[k : k + 1] + 0.5 * (part / D)
        new_cols_ref[k : k + 1] = new_cols
        cols_ref[k : k + 1] = new_cols
        line = jnp.where(lane == k, jnp.sum(part, axis=1, keepdims=True), line)
    block = jnp.concatenate([rows_ref[0:1], line, jnp.zeros((6, 128), F32)], axis=0)
    payload_ref[...] = jnp.broadcast_to(block[None], payload_ref.shape)


def step_kernel(received_ref, own_ref, kept_ref, half_moments_ref, new_cols_ref, step_ref, new_rows_ref):
    total = jnp.sum(received_ref[...], axis=0)
    diagonal = lax.broadcasted_iota(jnp.int32, (ROWS, ROWS), 0) == lax.broadcasted_iota(jnp.int32, (ROWS, ROWS), 1)
    for k in range(2):
        row_sum = total[0:1, k * ROWS : (k + 1) * ROWS]
        new_rows = half_moments_ref[k : k + 1] + 0.5 * (row_sum / FF)
        new_rows_ref[k : k + 1] = new_rows
        upright = jnp.sum(jnp.where(diagonal, new_rows, 0.0), axis=1, keepdims=True)
        row_level = 0.5 * (kept_ref[0:1, k : k + 1] / D) + 0.5 * (total[1:2, k : k + 1] / (FF * D))
        step_scale = jnp.sqrt(total[1:2, 2 + k : 3 + k] / (D * FF))
        estimate = upright * new_cols_ref[k : k + 1] / row_level
        step_ref[k] = step_scale * (own_ref[:, k * COLS : (k + 1) * COLS] * lax.rsqrt(estimate))


def call(kernel, out_shape, flops, *args, scratch=(), late=False):
    vmem = pl.BlockSpec(memory_space=pltpu.VMEM)
    smem = pl.BlockSpec(memory_space=pltpu.SMEM)
    specs = [smem if arg.dtype == jnp.int32 else vmem for arg in args]
    if late:
        specs[-1] = pl.BlockSpec(memory_space=pl.ANY)
    return pl.pallas_call(
        kernel,
        out_shape=out_shape,
        in_specs=specs,
        out_specs=jax.tree.map(lambda _: vmem, out_shape),
        scratch_shapes=scratch,
        compiler_params=pltpu.CompilerParams(vmem_limit_bytes=12 * 2**20),
        cost_estimate=pl.CostEstimate(flops=flops, bytes_accessed=4 * 2**20, transcendentals=0),
    )(*args)


def struct(shape, dtype=F32):
    return jax.ShapeDtypeStruct(shape, dtype)


def spread(values, axis, size):
    return lax.all_to_all(jnp.broadcast_to(values[None], (size,) + values.shape), axis, 0, 0, tiled=True)


def home_pairs(flip):
    pairs = []
    for yl in range(N_YL):
        for x in range(N_X):
            for yhi in range(N_YHI):
                swap = (yl + x) % 2
                target = ((yl ^ swap) * N_X + (x ^ swap)) * N_YHI + (yhi ^ flip)
                pairs.append(((yl * N_X + x) * N_YHI + yhi, target))
    return pairs


def x_shift(values, step):
    return lax.ppermute(values, "x", [(i, (i + step) % N_X) for i in range(N_X)])


def exchange(values, axis):
    return lax.ppermute(values, axis, [(0, 1), (1, 0)])


def shards(tokens, cotangent, weights, row_moments, col_moments):
    barrier = lax.optimization_barrier
    x, yhi, core, half_index = (lax.axis_index(name) for name in ("x", "yhi", "core", "yl"))
    place = jnp.stack([(x + half_index) % 2, x, yhi, core]).astype(jnp.int32)
    near = lax.ppermute(tokens, PLANE, home_pairs(0))
    far = lax.ppermute(tokens, PLANE, home_pairs(1))
    half = weights.astype(BF16)
    half = jnp.concatenate([half[0], half[1]], axis=1)
    pair_half = exchange(half, "yh")
    first = lax.axis_index("yh") == 0
    both = jnp.stack([jnp.where(first, half, pair_half), jnp.where(first, pair_half, half)])
    both, near = barrier((both, near))
    full = spread(both, "z", N_Z).reshape(N_Z // 2, 2, N_YH, ROWS, 2 * COLS)
    blocks = jnp.stack([near, far])
    blocks = jnp.stack([blocks] + [x_shift(blocks, step) for step in range(1, N_X)])
    others = exchange(blocks, "core")
    weight_squares = jnp.sum(weights * weights, axis=(1, 2))
    stats = jnp.concatenate([jnp.sum(row_moments, axis=1), weight_squares, jnp.zeros((124,), F32)]).reshape(1, 128)

    flops = 2 * TOK * (D // 2) * 2 * COLS
    wide = (TOK, 2 * COLS)
    grads_shape = (N_Z // 2, 2, N_YH, ROWS, 2 * COLS)
    for_pair = call(functools.partial(product_kernel, 1), struct(wide, BF16), flops, place, blocks, others, full)
    mine = call(functools.partial(product_kernel, 0), struct(wide), flops, place, blocks, others, full)
    summed = (mine + exchange(for_pair, "yl").astype(F32)) * SCALING
    gelu_value, gelu_slope = gelu_parts(summed[:, :COLS])
    hidden = jnp.concatenate(
        [
            (cotangent.astype(F32) * summed[:, COLS:] * gelu_slope).astype(BF16),
            (cotangent.astype(F32) * gelu_value).astype(BF16),
        ],
        axis=1,
    )
    pair_hidden = exchange(hidden, "yl")
    grads = call(grads_kernel, struct((2, 2, 2 * FEAT, 2 * COLS)), flops, place, blocks, others, hidden)
    grads = call(
        grads_sum_kernel, struct(grads_shape, BF16), flops, place, blocks, others, pair_hidden, grads
    )
    parts = lax.all_to_all(grads.reshape(N_Z, N_YH, ROWS, 2 * COLS), "z", 0, 0, tiled=True)
    parts = jnp.sum(parts.astype(F32), axis=0)
    own_part = jnp.where(first, parts[0], parts[1])
    parts = exchange(jnp.where(first, parts[1], parts[0]).astype(BF16), "yh")

    shape = struct((N_X, N_YHI, TOK, FEAT), BF16)
    terms, others = call(input_kernel, [shape, shape], 2 * flops, place, hidden, pair_hidden, full)
    terms = (terms.astype(F32) + exchange(others, "core").astype(F32)).astype(BF16)
    total = terms[0].astype(F32)
    for step in range(1, N_X):
        total = total + x_shift(terms[step], step).astype(F32)
    total = total.astype(BF16)
    near = lax.ppermute(total[0], PLANE, home_pairs(0))
    far = lax.ppermute(total[1], PLANE, home_pairs(1))
    parts, near = barrier((parts, near))
    input_grad = (near.astype(F32) + far.astype(F32)).astype(BF16)

    stats, half_moments, hidden = barrier((stats, 0.5 * row_moments, hidden))
    own, payload, rows = call(
        squares_kernel, [struct((ROWS, 2 * COLS)), struct((N_DP, 8, 128)), struct((8, 128))], 10**6, own_part, parts, stats
    )
    received = lax.all_to_all(payload, DP, 0, 0, tiled=True)
    payload, new_cols, kept, cols = call(
        columns_kernel,
        [struct((N_MP, 8, 128)), struct((2, COLS)), struct((1, 128)), struct((2, COLS))],
        10**6, received, rows, col_moments,
    )
    received = lax.all_to_all(payload, MP, 0, 0, tiled=True)
    weight_step, new_rows = call(
        step_kernel, [struct((2, ROWS, COLS)), struct((2, ROWS))], 10**6, received, own, kept, half_moments, cols
    )
    return (input_grad, weight_step, new_rows, new_cols)


def solution(mesh):
    fine = Mesh(mesh.devices.reshape(N_YH, N_YL, N_Z, N_X, N_YHI, N_CORE), DP + MP)
    return jax.shard_map(
        shards,
        mesh=fine,
        in_specs=(P(DP, MP), P(DP, MP), P(None, DP, MP), P(None, DP), P(None, MP)),
        out_specs=(P(DP, MP), P(None, DP, MP), P(None, DP), P(None, MP)),
        check_vma=False,
    )
```

```python
import functools
import jax
import jax.numpy as jnp
from jax import lax
from jax.experimental import pallas as pl
from jax.experimental.pallas import tpu as pltpu
from jax.sharding import Mesh, PartitionSpec as P

D = 2048
FF = 5120
N_YH, N_YL, N_Z, N_X, N_YHI, N_CORE = 2, 2, 8, 4, 2, 2
N_DP = N_YH * N_YL * N_Z
N_MP = N_X * N_YHI * N_CORE
N_GROUP = N_YH * N_Z
TOK = 368
ROWS = D // N_DP
COLS = FF // N_MP
FEAT = D // N_MP
SCALING = D ** (-0.5)
DP = ("yh", "yl", "z")
MP = ("x", "yhi", "core")
GROUP = ("yh", "z")
PLANE = ("yl", "x", "yhi")
F32 = jnp.float32
BF16 = jnp.bfloat16


def gelu_parts(values):
    cubed_values = values * values * values
    argument = 0.7978845608 * (values + 0.044715 * cubed_values)
    tangent = jnp.tanh(argument)
    gelu_value = 0.5 * values * (1.0 + tangent)
    gelu_slope = 0.5 * (1.0 + tangent) + 0.5 * values * (1.0 - tangent * tangent) * 0.7978845608 * (
        1.0 + 3.0 * 0.044715 * values * values
    )
    return (gelu_value, gelu_slope)


def token_pair(own_ref, other_ref, place_ref, group, i, j):
    d = (place_ref[0] + group) % 2 + 2 * i
    mine, other = own_ref[d, j], other_ref[d, j]
    return jnp.concatenate([mine, other], axis=1)


def weight_places(place_ref, group, i, j, sign):
    d = (place_ref[0] + group) % 2 + 2 * i
    row = ((place_ref[1] + sign * d + 4) % 4) // 2
    high = (place_ref[2] + j) % 2
    return row, 2 * high + place_ref[3], 2 * high + (place_ref[3] + 1) % 2


def weight_pair(w_ref, place_ref, group, i, j, sign):
    row, first, second = weight_places(place_ref, group, i, j, sign)
    return jnp.concatenate([w_ref[at, low, row] for at in (first, second) for low in range(2)], axis=0)


def product_kernel(group, place_ref, own_ref, other_ref, w_ref, out_ref):
    acc = None
    for i in range(2):
        for j in range(2):
            term = jnp.dot(
                token_pair(own_ref, other_ref, place_ref, group, i, j),
                weight_pair(w_ref, place_ref, group, i, j, -1),
                preferred_element_type=F32,
            )
            acc = term if acc is None else acc + term
    out_ref[...] = acc.astype(out_ref.dtype)


def hidden_kernel(mine_ref, cot_ref, received_any, hidden_ref, received_ref, sem):
    load = pltpu.make_async_copy(received_any, received_ref, sem)
    load.start()
    cot = cot_ref[...].astype(F32)
    load.wait()
    total = (mine_ref[...] + received_ref[...].astype(F32)) * SCALING
    gelu_value, gelu_slope = gelu_parts(total[:, :COLS])
    hidden_ref[:, :COLS] = (cot * total[:, COLS:] * gelu_slope).astype(BF16)
    hidden_ref[:, COLS:] = (cot * gelu_value).astype(BF16)


def grads_kernel(place_ref, own_ref, other_ref, hidden_ref, out_ref):
    hidden = hidden_ref[...]
    for i in range(2):
        for j in range(2):
            left = token_pair(own_ref, other_ref, place_ref, 0, i, j)
            product = lax.dot_general(left, hidden, (((0,), (0,)), ((), ())), preferred_element_type=F32)
            out_ref[i, j] = product


def grads_sum_kernel(place_ref, own_ref, other_ref, hidden_ref, mine_ref, out_ref):
    hidden = hidden_ref[...]
    for i in range(2):
        for j in range(2):
            left = token_pair(own_ref, other_ref, place_ref, 1, i, j)
            product = lax.dot_general(left, hidden, (((0,), (0,)), ((), ())), preferred_element_type=F32)
            row, first, second = weight_places(place_ref, 1, i, j, -1)
            mine_row = weight_places(place_ref, 0, 0, j, -1)[0]
            product = product + mine_ref[(mine_row + row) % 2, j]
            product = (product * SCALING).astype(BF16)
            out_ref[row, first] = product[:FEAT]
            out_ref[row, second] = product[FEAT:]


def input_kernel(place_ref, mine_ref, pair_ref, w_ref, own_ref, other_ref):
    for group in range(2):
        hidden = (pair_ref if group else mine_ref)[...]
        for i in range(2):
            for j in range(2):
                right = weight_pair(w_ref, place_ref, group, i, j, 1)
                product = lax.dot_general(hidden, right, (((1,), (1,)), ((), ())), preferred_element_type=F32)
                product = (product * SCALING).astype(BF16)
                e = (place_ref[0] + group) % 2 + 2 * i
                own_ref[e, j] = product[:, :FEAT]
                other_ref[e, j] = product[:, FEAT:]


def squares_kernel(parts_ref, stats_ref, own_ref, payload_ref, rows_ref):
    own = parts_ref[0].astype(F32)
    for part in range(1, N_GROUP):
        own = own + parts_ref[part].astype(F32)
    own_ref[...] = own
    squares = own * own + 1e-30
    cols = jnp.sum(squares, axis=0, keepdims=True)
    lines = [cols[:, 128 * i : 128 * (i + 1)] for i in range(5)]
    block = jnp.concatenate(lines + [stats_ref[...], jnp.zeros((2, 128), F32)], axis=0)
    payload_ref[...] = jnp.broadcast_to(block[None], payload_ref.shape)
    ones = jnp.ones((8, COLS), F32)
    for k in range(2):
        rows_ref[:, k * ROWS : (k + 1) * ROWS] = lax.dot_general(
            ones,
            squares[:, k * COLS : (k + 1) * COLS],
            (((1,), (1,)), ((), ())),
            precision=lax.Precision.HIGHEST,
            preferred_element_type=F32,
        )


def columns_kernel(received_ref, rows_ref, col_moments_ref, payload_ref, new_cols_ref, kept_ref, cols_ref):
    total = jnp.sum(received_ref[...], axis=0)
    cols = jnp.concatenate([total[i : i + 1] for i in range(5)], axis=1)
    kept = total[5:6]
    kept_ref[...] = kept
    lane = lax.broadcasted_iota(jnp.int32, (1, 128), 1)
    line = kept
    for k in range(2):
        part = cols[:, k * COLS : (k + 1) * COLS]
        new_cols = 0.5 * col_moments_ref[k : k + 1] + 0.5 * (part / D)
        new_cols_ref[k : k + 1] = new_cols
        cols_ref[k : k + 1] = new_cols
        line = jnp.where(lane == k, jnp.sum(part, axis=1, keepdims=True), line)
    block = jnp.concatenate([rows_ref[0:1], line, jnp.zeros((6, 128), F32)], axis=0)
    payload_ref[...] = jnp.broadcast_to(block[None], payload_ref.shape)


def step_kernel(received_ref, own_ref, kept_ref, half_moments_ref, new_cols_ref, step_ref, new_rows_ref):
    total = jnp.sum(received_ref[...], axis=0)
    diagonal = lax.broadcasted_iota(jnp.int32, (ROWS, ROWS), 0) == lax.broadcasted_iota(jnp.int32, (ROWS, ROWS), 1)
    for k in range(2):
        row_sum = total[0:1, k * ROWS : (k + 1) * ROWS]
        new_rows = half_moments_ref[k : k + 1] + 0.5 * (row_sum / FF)
        new_rows_ref[k : k + 1] = new_rows
        upright = jnp.sum(jnp.where(diagonal, new_rows, 0.0), axis=1, keepdims=True)
        row_level = 0.5 * (kept_ref[0:1, k : k + 1] / D) + 0.5 * (total[1:2, k : k + 1] / (FF * D))
        step_scale = jnp.sqrt(total[1:2, 2 + k : 3 + k] / (D * FF))
        estimate = upright * new_cols_ref[k : k + 1] / row_level
        step_ref[k] = step_scale * (own_ref[:, k * COLS : (k + 1) * COLS] * lax.rsqrt(estimate))


def call(kernel, out_shape, flops, *args, scratch=(), late=False):
    vmem = pl.BlockSpec(memory_space=pltpu.VMEM)
    smem = pl.BlockSpec(memory_space=pltpu.SMEM)
    specs = [smem if arg.dtype == jnp.int32 else vmem for arg in args]
    if late:
        specs[-1] = pl.BlockSpec(memory_space=pl.ANY)
    return pl.pallas_call(
        kernel,
        out_shape=out_shape,
        in_specs=specs,
        out_specs=jax.tree.map(lambda _: vmem, out_shape),
        scratch_shapes=scratch,
        compiler_params=pltpu.CompilerParams(vmem_limit_bytes=12 * 2**20),
        cost_estimate=pl.CostEstimate(flops=flops, bytes_accessed=4 * 2**20, transcendentals=0),
    )(*args)


def struct(shape, dtype=F32):
    return jax.ShapeDtypeStruct(shape, dtype)


def spread(values, axis, size):
    return lax.all_to_all(jnp.broadcast_to(values[None], (size,) + values.shape), axis, 0, 0, tiled=True)


def home_pairs(flip):
    pairs = []
    for yl in range(N_YL):
        for x in range(N_X):
            for yhi in range(N_YHI):
                swap = (yl + x) % 2
                target = ((yl ^ swap) * N_X + (x ^ swap)) * N_YHI + (yhi ^ flip)
                pairs.append(((yl * N_X + x) * N_YHI + yhi, target))
    return pairs


def x_shift(values, step):
    return lax.ppermute(values, "x", [(i, (i + step) % N_X) for i in range(N_X)])


def exchange(values, axis):
    return lax.ppermute(values, axis, [(0, 1), (1, 0)])


def shards(tokens, cotangent, weights, row_moments, col_moments):
    barrier = lax.optimization_barrier
    x, yhi, core, half_index = (lax.axis_index(name) for name in ("x", "yhi", "core", "yl"))
    place = jnp.stack([(x + half_index) % 2, x, yhi, core]).astype(jnp.int32)
    near = lax.ppermute(tokens, PLANE, home_pairs(0))
    far = lax.ppermute(tokens, PLANE, home_pairs(1))
    half = weights.astype(BF16)
    half = jnp.concatenate([half[0], half[1]], axis=1)
    pair_half = exchange(half, "yh")
    first = lax.axis_index("yh") == 0
    both = jnp.stack([jnp.where(first, half, pair_half), jnp.where(first, pair_half, half)])
    both, near = barrier((both, near))
    full = spread(both, "z", N_Z).reshape(N_Z // 2, 2, N_YH, ROWS, 2 * COLS)
    blocks = jnp.stack([near, far])
    blocks = jnp.stack([blocks] + [x_shift(blocks, step) for step in range(1, N_X)])
    others = exchange(blocks, "core")
    weight_squares = jnp.sum(weights * weights, axis=(1, 2))
    stats = jnp.concatenate([jnp.sum(row_moments, axis=1), weight_squares, jnp.zeros((124,), F32)]).reshape(1, 128)

    flops = 2 * TOK * (D // 2) * 2 * COLS
    wide = (TOK, 2 * COLS)
    grads_shape = (N_YH, N_X, 2 * ROWS, 2 * COLS)
    for_pair = call(functools.partial(product_kernel, 1), struct(wide, BF16), flops, place, blocks, others, full)
    mine = call(functools.partial(product_kernel, 0), struct(wide), flops, place, blocks, others, full)
    summed = (mine + exchange(for_pair, "yl").astype(F32)) * SCALING
    gelu_value, gelu_slope = gelu_parts(summed[:, :COLS])
    hidden = jnp.concatenate(
        [
            (cotangent.astype(F32) * summed[:, COLS:] * gelu_slope).astype(BF16),
            (cotangent.astype(F32) * gelu_value).astype(BF16),
        ],
        axis=1,
    )
    pair_hidden = exchange(hidden, "yl")
    grads = call(grads_kernel, struct((2, 2, 2 * FEAT, 2 * COLS)), flops, place, blocks, others, hidden)
    grads = call(
        grads_sum_kernel, struct(grads_shape, BF16), flops, place, blocks, others, pair_hidden, grads
    )
    parts = lax.all_to_all(grads.reshape(N_GROUP, ROWS, 2 * COLS), GROUP, 0, 0, tiled=True)

    shape = struct((N_X, N_YHI, TOK, FEAT), BF16)
    terms, others = call(input_kernel, [shape, shape], 2 * flops, place, hidden, pair_hidden, full)
    terms = (terms.astype(F32) + exchange(others, "core").astype(F32)).astype(BF16)
    total = terms[0].astype(F32)
    for step in range(1, N_X):
        total = total + x_shift(terms[step], step).astype(F32)
    total = total.astype(BF16)
    near = lax.ppermute(total[0], PLANE, home_pairs(0))
    far = lax.ppermute(total[1], PLANE, home_pairs(1))
    parts, near = barrier((parts, near))

    stats, half_moments, hidden = barrier((stats, 0.5 * row_moments, hidden))
    own, payload, rows = call(
        squares_kernel, [struct((ROWS, 2 * COLS)), struct((N_DP, 8, 128)), struct((8, 128))], 10**6, parts, stats
    )
    received = lax.all_to_all(payload, DP, 0, 0, tiled=True)
    payload, new_cols, kept, cols = call(
        columns_kernel,
        [struct((N_MP, 8, 128)), struct((2, COLS)), struct((1, 128)), struct((2, COLS))],
        10**6, received, rows, col_moments,
    )
    received = lax.all_to_all(payload, MP, 0, 0, tiled=True)
    received, near, far = barrier((received, near, far))
    input_grad = (near.astype(F32) + far.astype(F32)).astype(BF16)
    weight_step, new_rows = call(
        step_kernel, [struct((2, ROWS, COLS)), struct((2, ROWS))], 10**6, received, own, kept, half_moments, cols
    )
    return (input_grad, weight_step, new_rows, new_cols)


def solution(mesh):
    fine = Mesh(mesh.devices.reshape(N_YH, N_YL, N_Z, N_X, N_YHI, N_CORE), DP + MP)
    return jax.shard_map(
        shards,
        mesh=fine,
        in_specs=(P(DP, MP), P(DP, MP), P(None, DP, MP), P(None, DP), P(None, MP)),
        out_specs=(P(DP, MP), P(None, DP, MP), P(None, DP), P(None, MP)),
        check_vma=False,
    )
```
